512 devices in a mesh: seq: 32 (over y_lo, z, core), grp: 16 (over y_hi, x).
Axes of the slice: x: 4, y: 8 (y_hi: 4, y_lo: 2; y = y_hi * 2 + y_lo), z: 8, core: 2. Of those that a mesh axis runs over, the one named last changes fastest.
Arguments:
- text_q: bfloat16 [16, 8192, 1024], P('grp', 'seq'), may hold values from -6 to 6
- cross_q: bfloat16 [16, 8192, 1024], P('grp', 'seq'), may hold values from -6 to 6
- text_k: bfloat16 [16, 8192, 128], P('grp', 'seq'), may hold values from -6 to 6
- text_v: bfloat16 [16, 8192, 128], P('grp', 'seq'), may hold values from -12 to 12
- frame_k: bfloat16 [16, 512, 128], P('grp', 'seq'), may hold values from -6 to 6
- frame_v: bfloat16 [16, 512, 128], P('grp', 'seq'), may hold values from -12 to 12
- block_pos: int32 [32], replicated, may hold values from 0 to 31, each once
- frame_mask: int32 [32, 16], replicated, may hold values from 0 to 1, as said below
Outputs:
- self_out: bfloat16 [16, 8192, 1024], P('grp', 'seq')
- cross_out: bfloat16 [16, 8192, 1024], P('grp', 'seq')
The draws below stay inside these ranges and needn't reach their ends.
Inputs may be any that keep to these rules, and one draw needn't show every extreme that they name: `frame_mask`: every row has at least one 1.
All inputs are finite; a program needn't handle non-finite values.
Results may differ from the reference program's by a relative error of at most 0.008.
Values may be sent and summed in bfloat16 or wider, within the bound.
No kernel may reach another device: no remote copies, remote signals or barrier semaphores. Data moves between devices by JAX's collectives and lax.ppermute only.
A program may use at most 64 MiB of HBM per device.

```python
import jax
import jax.numpy as jnp
from jax import lax

H = 8
DH = 128
TOK_DEV = 256
TEXT = 8192
BLOCKS = 32
SLABS = 16
FRAMES = 16
FTOK = 512


def draw_text_q(key, part):
    key = jax.random.fold_in(key, 11)
    shape = (SLABS, TEXT, H * DH)
    values = jnp.clip(jax.random.normal(key, shape, jnp.float32), -6.0, 6.0)
    return values.astype(jnp.bfloat16)


def draw_cross_q(key, part):
    key = jax.random.fold_in(key, 12)
    shape = (SLABS, TEXT, H * DH)
    values = jnp.clip(jax.random.normal(key, shape, jnp.float32), -6.0, 6.0)
    return values.astype(jnp.bfloat16)


def draw_text_k(key, part):
    key = jax.random.fold_in(key, 13)
    shape = (SLABS, TEXT, DH)
    values = jnp.clip(jax.random.normal(key, shape, jnp.float32), -6.0, 6.0)
    return values.astype(jnp.bfloat16)


def draw_frame_k(key, part):
    key = jax.random.fold_in(key, 14)
    shape = (FRAMES, FTOK, DH)
    values = jnp.clip(jax.random.normal(key, shape, jnp.float32), -6.0, 6.0)
    return values.astype(jnp.bfloat16)


def draw_frame_mask(key, part):
    key = jax.random.fold_in(key, 15)
    first_key, second_key = jax.random.split(key)
    extra = jax.random.randint(first_key, (BLOCKS, FRAMES), 0, 4) == 0
    forced = jax.random.randint(second_key, (BLOCKS,), 0, FRAMES)
    chosen = jnp.arange(FRAMES)[None, :] == forced[:, None]
    return jnp.logical_or(extra, chosen).astype(jnp.int32)


def levels(rng, extent, shards, low, largest):
    level = 1.0
    for dim, parts in shards:
        steps = jax.random.uniform(jax.random.fold_in(jax.random.fold_in(rng, 6), dim), (parts,), jnp.float32, low / len(shards), largest / len(shards))
        level = level * jnp.repeat(jnp.exp(steps), extent[dim] // parts).reshape((-1,) + (1,) * (len(extent) - 1 - dim))
    return level


def setup_inputs(seed: int = 0) -> dict:
    key_of = jax.random.split(jax.random.key(seed), 9)
    text_q = draw_text_q(jax.random.fold_in(key_of[8], 71), 0)
    cross_q = draw_cross_q(jax.random.fold_in(key_of[8], 71), 0)
    text_k = draw_text_k(jax.random.fold_in(key_of[8], 71), 0)
    text_v = jnp.clip(jax.random.uniform(key_of[3], (SLABS, TEXT, DH), jnp.float32, -12.0, 12.0) * levels(key_of[3], (SLABS, TEXT, DH), ((0, 16), (1, 32)), -0.4, 0.0), -12.0, 12.0).astype(jnp.bfloat16)
    frame_k = draw_frame_k(jax.random.fold_in(key_of[8], 71), 0)
    frame_v = jnp.clip(jax.random.uniform(key_of[5], (FRAMES, FTOK, DH), jnp.float32, -12.0, 12.0) * levels(key_of[5], (FRAMES, FTOK, DH), ((0, 16), (1, 32)), -0.4, 0.0), -12.0, 12.0).astype(jnp.bfloat16)
    block_pos = jax.random.permutation(key_of[6], BLOCKS).astype(jnp.int32)
    frame_mask = draw_frame_mask(jax.random.fold_in(key_of[8], 71), 0)
    return dict(text_q=text_q, cross_q=cross_q, text_k=text_k, text_v=text_v, frame_k=frame_k, frame_v=frame_v, block_pos=block_pos, frame_mask=frame_mask)


def attend_block(queries, key_rows, value_rows, allowed, factor):
    scores = jnp.einsum('thd,kd->thk', queries.astype(jnp.float32), key_rows.astype(jnp.float32)) * factor
    scores = jnp.where(allowed[:, None, :], scores, jnp.float32(-1e30))
    row_max = jnp.max(scores, axis=-1, keepdims=True)
    weights = jnp.where(allowed[:, None, :], jnp.exp(scores - row_max), jnp.float32(0.0))
    row_sum = jnp.sum(weights, axis=-1)
    rounded = lax.optimization_barrier(weights.astype(jnp.bfloat16)).astype(jnp.float32)
    mixed = jnp.einsum('thk,kd->thd', rounded, value_rows.astype(jnp.float32))
    result = mixed / row_sum[..., None]
    return result.reshape(result.shape[0], -1).astype(jnp.bfloat16)


def reference(text_q, cross_q, text_k, text_v, frame_k, frame_v, block_pos, frame_mask):
    factor = DH ** -0.5
    rows_all = jnp.arange(TEXT, dtype=jnp.int32)
    positions = block_pos[rows_all // TOK_DEV] * TOK_DEV + rows_all % TOK_DEV
    flat_k = frame_k.reshape(FRAMES * FTOK, DH)
    flat_v = frame_v.reshape(FRAMES * FTOK, DH)
    frame_of_key = jnp.arange(FRAMES * FTOK, dtype=jnp.int32) // FTOK

    def one_block(index):
        slab = index // BLOCKS
        block = index % BLOCKS
        first = (block * TOK_DEV).astype(jnp.int32)
        zero = jnp.int32(0)
        queries = lax.dynamic_slice(text_q, (slab, first, zero), (1, TOK_DEV, H * DH))[0].reshape(TOK_DEV, H, DH)
        cross_rows = lax.dynamic_slice(cross_q, (slab, first, zero), (1, TOK_DEV, H * DH))[0].reshape(TOK_DEV, H, DH)
        key_rows = lax.dynamic_index_in_dim(text_k, slab, 0, keepdims=False)
        value_rows = lax.dynamic_index_in_dim(text_v, slab, 0, keepdims=False)
        query_pos = lax.dynamic_slice_in_dim(positions, first, TOK_DEV)
        causal = positions[None, :] <= query_pos[:, None]
        self_part = attend_block(queries, key_rows, value_rows, causal, factor)
        seen = frame_mask[block_pos[block]] > 0
        allowed = jnp.broadcast_to(seen[frame_of_key][None, :], (TOK_DEV, FRAMES * FTOK))
        cross_part = attend_block(cross_rows, flat_k, flat_v, allowed, factor)
        return self_part, cross_part

    self_parts, cross_parts = lax.map(one_block, jnp.arange(SLABS * BLOCKS, dtype=jnp.int32))
    self_out = self_parts.reshape(SLABS, TEXT, H * DH)
    cross_out = cross_parts.reshape(SLABS, TEXT, H * DH)
    return self_out, cross_out
```

```python
import jax
import jax.numpy as jnp
from jax import lax
from jax.experimental import pallas as pl
from jax.experimental.pallas import tpu as pltpu
from jax.sharding import PartitionSpec as P

H = 8
DH = 128
ROWS = 256
ONES = 16
FACTOR = DH**-0.5
FACTOR2 = FACTOR * 1.4426950408889634
LOW, HIGH = 1e-28, 1e28
F32, BF16 = jnp.float32, jnp.bfloat16

Y, Z, CORES = 2, 8, 2
YH, X = 4, 4


def seq_id(y, z, c):
    return (y % Y * Z + z % Z) * CORES + c % CORES


ZC_GROUPS = [[seq_id(y, z, c) for z in range(Z) for c in range(CORES)] for y in range(Y)]
YZ_GROUPS = [[seq_id(y, z, c) for y in range(Y) for z in range(Z)] for c in range(CORES)]
YH_GROUPS = [[y * X + x for y in range(YH)] for x in range(X)]
TO_Y = [(seq_id(y, z, c), seq_id(y + 1, z, c)) for y in range(Y) for z in range(Z) for c in range(CORES)]
TO_CORE = [(seq_id(y, z, c), seq_id(y, z, c + 1)) for y in range(Y) for z in range(Z) for c in range(CORES)]


def to_x(steps):
    return [(y * X + x, y * X + (x + steps) % X) for y in range(YH) for x in range(X)]


def dot(a, b):
    return lax.dot_general(a, b, (((1,), (0,)), ((), ())), preferred_element_type=F32)


def causal():
    keys = lax.broadcasted_iota(jnp.int32, (ROWS, ROWS), 0)
    queries = lax.broadcasted_iota(jnp.int32, (ROWS, ROWS), 1)
    return keys <= queries


def add_keys(qt, acc, keys, values, masked=False, depth=2):
    ones = jnp.ones((ONES, keys.shape[0]), BF16)
    weights = jnp.concatenate([values.T, ones], axis=0)
    scores = [dot(keys, qt[h]) for h in range(depth)]
    for h in range(H):
        p = jnp.exp2(scores.pop(0) * FACTOR2)
        if masked:
            p = jnp.where(causal(), p, 0.0)
        p = p.astype(BF16)
        if h + depth < H:
            scores.append(dot(keys, qt[h + depth]))
        acc[h] += dot(weights, p)


def safe_attention(qt, acc, top, read, parts, own):
    acc[...] = jnp.zeros_like(acc)

    def scores_of(keys, h, masked):
        s = dot(keys, qt[h]) * FACTOR
        return jnp.where(causal(), s, -1e30) if masked else s

    def find(keys, masked):
        def head(h, _):
            s = scores_of(keys, h, masked)
            top[h] = jnp.maximum(top[h], jnp.max(s, axis=0, keepdims=True))
            return 0

        lax.fori_loop(0, H, head, 0)

    def add(keys, values, masked):
        weights = jnp.concatenate([values.T, jnp.ones((ONES, keys.shape[0]), BF16)], axis=0)

        def head(h, _):
            p = jnp.exp(scores_of(keys, h, masked) - top[h])
            acc[h] += dot(weights, p.astype(BF16))
            return 0

        lax.fori_loop(0, H, head, 0)

    top[...] = jnp.full_like(top, -1e30)

    def first(j, _):
        find(read(j)[0], False)
        return 0

    def second(j, _):
        add(*read(j), False)
        return 0

    lax.fori_loop(0, parts, first, 0)
    if own is not None:
        find(own[0][...], True)
    lax.fori_loop(0, parts, second, 0)
    if own is not None:
        add(own[0][...], own[1][...], True)


def run(q_ref, o_ref, qt, acc, top, chosen, parts, read, group, own):
    for h in range(H):
        qt[h] = q_ref[:, h * DH : (h + 1) * DH].T
    acc[...] = jnp.zeros_like(acc)

    def several(first, number):
        pairs = [read(chosen[first + i]) for i in range(number)]
        return tuple(jnp.concatenate(x, axis=0) for x in zip(*pairs))

    def whole(i, _):
        add_keys(qt, acc, *several(i * group, group))
        return 0

    if own is not None:
        add_keys(qt, acc, own[0][...], own[1][...], masked=True, depth=4)
    lax.fori_loop(0, parts // group, whole, 0)
    size = group // 2
    while size:
        @pl.when(parts // size % 2 == 1)
        def _(size=size):
            add_keys(qt, acc, *several(parts // (2 * size) * (2 * size), size), depth=4)

        size //= 2

    sums = acc[:, DH : DH + 1, :]
    good = jnp.logical_and(sums > LOW, sums < HIGH)
    worst = jnp.min(jnp.where(good, 1.0, 0.0))

    @pl.when(worst < 0.5)
    def _():
        safe_attention(qt, acc, top, lambda j: read(chosen[j]), parts, own)

    for h in range(H):
        o_ref[:, h * DH : (h + 1) * DH] = (acc[h, :DH] / acc[h, DH : DH + 1]).astype(BF16).T


def self_kernel(place, block_pos, q_ref, kv, o_ref, qt, acc, top, chosen):
    me = place[0]
    mine = block_pos[me]
    my_y, my_zc = me // (Z * CORES), me % (Z * CORES)

    def listed(i, count):
        zc, other = i // Y, i % Y
        source = (my_y + other) % Y * (Z * CORES) + zc
        keep = block_pos[source] < mine

        @pl.when(keep)
        def _():
            chosen[count] = i

        return count + keep.astype(jnp.int32)

    parts = lax.fori_loop(0, Y * Z * CORES, listed, 0)

    def read(i):
        return kv[i // Y, i % Y, 0], kv[i // Y, i % Y, 1]

    run(q_ref, o_ref, qt, acc, top, chosen, parts, read, 4, (kv.at[my_zc, 0, 0], kv.at[my_zc, 0, 1]))


def cross_kernel(place, block_pos, mask, q_ref, mine_ref, other_ref, o_ref, qt, acc, top, chosen):
    row = block_pos[place[0]]
    my_x = place[1] % X

    def listed(i, count):
        slot, y = i // YH, i % YH
        shift = jnp.where(slot == 0, 0, jnp.where(slot == 1, X - 1, jnp.where(slot == 2, 1, 2)))
        keep = mask[row, y * X + (my_x + shift) % X] > 0

        @pl.when(keep)
        def _():
            chosen[count] = i

        return count + keep.astype(jnp.int32)

    parts = lax.fori_loop(0, X * YH, listed, 0)

    def read(i):
        halves = [ref[i // YH, i % YH] for ref in (mine_ref, other_ref)]
        return tuple(
            jnp.concatenate([half[:, which].reshape(-1, DH) for half in halves], axis=0) for which in (0, 1)
        )

    run(q_ref, o_ref, qt, acc, top, chosen, parts, read, 2, None)


def call(kernel, name, scalars, arrays, parts):
    return pl.pallas_call(
        kernel,
        out_shape=jax.ShapeDtypeStruct((ROWS, H * DH), BF16),
        in_specs=[pl.BlockSpec(memory_space=pltpu.SMEM)] * len(scalars)
        + [pl.BlockSpec(memory_space=pltpu.VMEM)] * len(arrays),
        out_specs=pl.BlockSpec(memory_space=pltpu.VMEM),
        scratch_shapes=[
            pltpu.VMEM((H, DH, ROWS), BF16),
            pltpu.VMEM((H, DH + ONES, ROWS), F32),
            pltpu.VMEM((H, 1, ROWS), F32),
            pltpu.SMEM((parts,), jnp.int32),
        ],
        compiler_params=pltpu.CompilerParams(vmem_limit_bytes=40 * 2**20),
        cost_estimate=pl.CostEstimate(
            flops=16 * 4 * H * ROWS * ROWS * DH, bytes_accessed=6 * 2**20, transcendentals=16 * H * ROWS * ROWS
        ),
        name=name,
    )(*scalars, *arrays)


def per_device(text_q, cross_q, text_k, text_v, frame_k, frame_v, block_pos, frame_mask):
    place = jnp.stack([lax.axis_index("seq"), lax.axis_index("grp")]).astype(jnp.int32)

    own = jnp.stack([text_k[0], text_v[0]])
    across = lax.ppermute(own, "seq", TO_Y)
    text = lax.all_gather(jnp.stack([own, across]), "seq", axis_index_groups=ZC_GROUPS)

    piece = jnp.stack([frame_k[0], frame_v[0]])
    frame = lax.all_to_all(
        jnp.broadcast_to(piece, (Y * Z, *piece.shape)), "seq", 0, 0, axis_index_groups=YZ_GROUPS
    )
    column = lax.all_to_all(jnp.broadcast_to(frame, (YH, *frame.shape)), "grp", 0, 0, axis_index_groups=YH_GROUPS)
    columns = [column] + [lax.ppermute(column, "grp", to_x(steps)) for steps in (1, -1, 2)]
    half = jnp.stack(columns)
    other_half = lax.ppermute(half, "seq", TO_CORE)

    cross_out = call(
        cross_kernel, "cross", [place, block_pos, frame_mask], [cross_q[0], half, other_half], X * YH
    )
    self_out = call(self_kernel, "own", [place, block_pos], [text_q[0], text], Y * Z * CORES)
    return self_out[None], cross_out[None]


def solution(mesh):
    rows = P("grp", "seq", None)
    return jax.shard_map(
        per_device,
        mesh=mesh,
        in_specs=(rows, rows, rows, rows, rows, rows, P(), P()),
        out_specs=(rows, rows),
        check_vma=False,
    )
```

```python
import functools

import jax
import jax.numpy as jnp
from jax import lax
from jax.experimental import pallas as pl
from jax.experimental.pallas import tpu as pltpu
from jax.sharding import PartitionSpec as P

H = 8
DH = 128
ROWS = 256
ONES = 16
FACTOR = DH**-0.5
FACTOR2 = FACTOR * 1.4426950408889634
LOW, HIGH = 1e-28, 1e28
F32, BF16 = jnp.float32, jnp.bfloat16

Y, Z, CORES = 2, 8, 2
YH, X = 4, 4
GROUP = 4
COLUMN_SHIFTS = (0, -1, 1, 2)


def seq_id(y, z, c):
    return (y % Y * Z + z % Z) * CORES + c % CORES


Z_GROUPS = [[seq_id(y, z, c) for z in range(Z)] for y in range(Y) for c in range(CORES)]
PLANE_GROUPS = [
    [(yh * X + x) * (Y * Z * CORES) + seq_id(y, z, c) for yh in range(YH) for y in range(Y) for z in range(Z)]
    for x in range(X)
    for c in range(CORES)
]
TO_Y = [(seq_id(y, z, c), seq_id(y + 1, z, c)) for y in range(Y) for z in range(Z) for c in range(CORES)]
TO_CORE = [(seq_id(y, z, c), seq_id(y, z, c + 1)) for y in range(Y) for z in range(Z) for c in range(CORES)]


def to_x(steps):
    return [(y * X + x, y * X + (x + steps) % X) for y in range(YH) for x in range(X)]


def dot(a, b):
    return lax.dot_general(a, b, (((1,), (0,)), ((), ())), preferred_element_type=F32)


def causal():
    keys = lax.broadcasted_iota(jnp.int32, (ROWS, ROWS), 0)
    queries = lax.broadcasted_iota(jnp.int32, (ROWS, ROWS), 1)
    return keys <= queries


def weights_of(values):
    return jnp.concatenate([values.T, jnp.ones((ONES, values.shape[0]), BF16)], axis=0)


def add_keys(qt, acc, keys, values, masked=False, depth=2):
    weights = weights_of(values)
    scores = [dot(keys, qt[h]) for h in range(depth)]
    for h in range(H):
        p = jnp.exp2(scores.pop(0) * FACTOR2)
        if masked:
            p = jnp.where(causal(), p, 0.0)
        p = p.astype(BF16)
        if h + depth < H:
            scores.append(dot(keys, qt[h + depth]))
        acc[h] += dot(weights, p)


def safe_attention(qt, acc, top, read, parts, own):
    acc[...] = jnp.zeros_like(acc)
    top[...] = jnp.full_like(top, -1e30)

    def scores_of(keys, h, masked):
        s = dot(keys, qt[h]) * FACTOR
        return jnp.where(causal(), s, -1e30) if masked else s

    def find(keys, values, masked):
        def head(h, _):
            s = scores_of(keys, h, masked)
            top[h] = jnp.maximum(top[h], jnp.max(s, axis=0, keepdims=True))
            return 0

        lax.fori_loop(0, H, head, 0)

    def add(keys, values, masked):
        weights = weights_of(values)

        def head(h, _):
            p = jnp.exp(scores_of(keys, h, masked) - top[h])
            acc[h] += dot(weights, p.astype(BF16))
            return 0

        lax.fori_loop(0, H, head, 0)

    for visit in (find, add):
        def one(j, _, visit=visit):
            visit(*read(j, 1), False)
            return 0

        lax.fori_loop(0, parts, one, 0)
        if own is not None:
            visit(own[0][...], own[1][...], True)


def attend(q_ref, acc, qt, top, parts, read, own):
    for h in range(H):
        qt[h] = q_ref[:, h * DH : (h + 1) * DH].T
    acc[...] = jnp.zeros_like(acc)
    top[...] = jnp.zeros_like(top)
    if own is not None:
        add_keys(qt, acc, own[0][...], own[1][...], masked=True, depth=4)

    def whole(i, _):
        add_keys(qt, acc, *read(i * GROUP, GROUP))
        return 0

    lax.fori_loop(0, parts // GROUP, whole, 0)
    size = GROUP // 2
    while size:
        @pl.when(parts // size % 2 == 1)
        def _(size=size):
            add_keys(qt, acc, *read(parts // (2 * size) * (2 * size), size), depth=4)

        size //= 2

    if own is None:
        @pl.when(parts == 0)
        def _():
            top[...] = jnp.full_like(top, -1e30)

    sums = acc[:, DH : DH + 1, :]
    good = jnp.logical_and(sums > LOW, sums < HIGH)
    worst = jnp.min(jnp.where(good, 1.0, 0.0))
    some = parts >= (1 if own is None else 0)

    @pl.when(jnp.logical_and(worst < 0.5, some))
    def _():
        safe_attention(qt, acc, top, read, parts, own)

    for h in range(H):
        acc[h, DH + ONES // 2 :] = jnp.broadcast_to(top[h], (ONES // 2, ROWS))


def list_blocks(place, block_pos, chosen, rows_of):
    me = place[0]
    my_y, my_core = me // (Z * CORES), me % CORES

    def listed(i, count):
        source = (my_y + i % Y) % Y * (Z * CORES) + i // Y * CORES + my_core
        keep = block_pos[source] < block_pos[rows_of]

        @pl.when(keep)
        def _():
            chosen[count] = i

        return count + keep.astype(jnp.int32)

    return lax.fori_loop(0, Y * Z, listed, 0)


def self_kernel(place, block_pos, q_ref, partner_ref, kv, mine, theirs, qt, top, chosen):
    def read(first, number):
        blocks = [chosen[first + i] for i in range(number)]
        return tuple(jnp.concatenate([kv[b // Y, b % Y, which] for b in blocks], axis=0) for which in (0, 1))

    me = place[0]
    partner = me + 1 - 2 * (me % CORES)
    attend(partner_ref, theirs, qt, top, list_blocks(place, block_pos, chosen, partner), read, None)
    my_z = me // CORES % Z
    own = (kv.at[my_z, 0, 0], kv.at[my_z, 0, 1])
    attend(q_ref, mine, qt, top, list_blocks(place, block_pos, chosen, me), read, own)


def cross_kernel(partner, place, block_pos, mask, q_ref, *refs):
    columns, (out, qt, top, keys, values) = refs[:X], refs[X:]
    me = place[0]
    row = block_pos[me + 1 - 2 * (me % CORES) if partner else me]
    my_x = place[1] % X
    parts = jnp.int32(0)
    for column, shift in zip(columns, COLUMN_SHIFTS):
        for y in range(YH):
            keep = mask[row, y * X + (my_x + shift) % X] > 0

            @pl.when(keep)
            def _(column=column, y=y, parts=parts):
                at = pl.ds(pl.multiple_of(parts * ROWS, ROWS), ROWS)
                keys[at] = column[y, :, 0].reshape(ROWS, DH)
                values[at] = column[y, :, 1].reshape(ROWS, DH)

            parts = parts + keep.astype(jnp.int32)

    def read(first, number):
        at = pl.ds(pl.multiple_of(first * ROWS, ROWS), number * ROWS)
        return keys[at], values[at]

    attend(q_ref, out, qt, top, parts, read, None)


def join_kernel(mine, theirs, o_ref):
    for h in range(H):
        shifts = [part[h, DH + ONES // 2 : DH + ONES // 2 + 1] for part in (mine, theirs)]
        common = jnp.maximum(*shifts)
        scales = [jnp.exp(shift - common) for shift in shifts]
        total = sum(part[h, DH : DH + 1] * scale for part, scale in zip((mine, theirs), scales))
        rows = sum(part[h, :DH] * (scale / total) for part, scale in zip((mine, theirs), scales))
        o_ref[:, h * DH : (h + 1) * DH] = rows.astype(BF16).T


SUMS = jax.ShapeDtypeStruct((H, DH + ONES, ROWS), F32)
WORK = [pltpu.VMEM((H, DH, ROWS), BF16), pltpu.VMEM((H, 1, ROWS), F32)]


def call(kernel, name, scalars, arrays, outs, scratch, units):
    return pl.pallas_call(
        kernel,
        out_shape=outs,
        in_specs=[pl.BlockSpec(memory_space=pltpu.SMEM)] * len(scalars)
        + [pl.BlockSpec(memory_space=pltpu.VMEM)] * len(arrays),
        out_specs=jax.tree.map(lambda _: pl.BlockSpec(memory_space=pltpu.VMEM), outs),
        scratch_shapes=scratch,
        compiler_params=pltpu.CompilerParams(vmem_limit_bytes=32 * 2**20),
        cost_estimate=pl.CostEstimate(
            flops=units * 8 * H * ROWS * ROWS * DH, bytes_accessed=4 * 2**20, transcendentals=units * H * ROWS * ROWS
        ),
        name=name,
    )(*scalars, *arrays)


def per_device(text_q, cross_q, text_k, text_v, frame_k, frame_v, block_pos, frame_mask):
    place = jnp.stack([lax.axis_index("seq"), lax.axis_index("grp")]).astype(jnp.int32)

    own = jnp.stack([text_k[0], text_v[0]])
    across = lax.ppermute(own, "seq", TO_Y)
    partner_q = lax.ppermute(text_q[0], "seq", TO_CORE)
    partner_cross_q = lax.ppermute(cross_q[0], "seq", TO_CORE)
    text = lax.all_gather(jnp.stack([own, across]), "seq", axis_index_groups=Z_GROUPS)

    piece = jnp.stack([frame_k[0], frame_v[0]])
    plane = lax.all_to_all(
        jnp.broadcast_to(piece, (YH * Y * Z, *piece.shape)), ("grp", "seq"), 0, 0, axis_index_groups=PLANE_GROUPS
    )
    column = plane.reshape(YH, Y * Z, *piece.shape)
    columns = [column] + [lax.ppermute(column, "grp", to_x(-shift)) for shift in COLUMN_SHIFTS[1:]]

    mine, theirs = call(
        self_kernel, "own", [place, block_pos], [text_q[0], partner_q, text], (SUMS, SUMS),
        [*WORK, pltpu.SMEM((Y * Z,), jnp.int32)], 16,
    )
    self_theirs = lax.ppermute(theirs, "seq", TO_CORE)

    def cross(queries, partner):
        return call(
            functools.partial(cross_kernel, partner), "cross", [place, block_pos, frame_mask], [queries, *columns],
            SUMS, [*WORK, *[pltpu.VMEM((X * YH * ROWS, DH), BF16)] * 2], 5,
        )

    partner_cross_q, mine = lax.optimization_barrier((partner_cross_q, mine))
    cross_theirs = cross(partner_cross_q, True)
    own_cross_q, cross_theirs = lax.optimization_barrier((cross_q[0], cross_theirs))
    cross_theirs = lax.ppermute(cross_theirs, "seq", TO_CORE)
    cross_mine = cross(own_cross_q, False)

    def join(a, b):
        return call(join_kernel, "join", [], [a, b], jax.ShapeDtypeStruct((ROWS, H * DH), BF16), [], 1)

    self_out = join(mine, self_theirs)
    cross_out = join(cross_mine, cross_theirs)
    return self_out[None], cross_out[None]


def solution(mesh):
    rows = P("grp", "seq", None)
    return jax.shard_map(
        per_device,
        mesh=mesh,
        in_specs=(rows, rows, rows, rows, rows, rows, P(), P()),
        out_specs=(rows, rows),
        check_vma=False,
    )
```

```python
import functools

import jax
import jax.numpy as jnp
from jax import lax
from jax.experimental import pallas as pl
from jax.experimental.pallas import tpu as pltpu
from jax.sharding import PartitionSpec as P

H = 8
DH = 128
ROWS = 256
ONES = 16
FACTOR = DH**-0.5
FACTOR2 = FACTOR * 1.4426950408889634
LOW, HIGH = 1e-28, 1e28
F32, BF16 = jnp.float32, jnp.bfloat16

Y, Z, CORES = 2, 8, 2
YH, X = 4, 4
GROUP = 4
COLUMN_SHIFTS = (0, -1, 1, 2)


def seq_id(y, z, c):
    return (y % Y * Z + z % Z) * CORES + c % CORES


Z_GROUPS = [[seq_id(y, z, c) for z in range(Z)] for y in range(Y) for c in range(CORES)]
Y_GROUPS = [
    [(yh * X + x) * (Y * Z * CORES) + seq_id(y, z, c) for yh in range(YH) for y in range(Y)]
    for x in range(X)
    for z in range(Z)
    for c in range(CORES)
]
TO_Y = [(seq_id(y, z, c), seq_id(y + 1, z, c)) for y in range(Y) for z in range(Z) for c in range(CORES)]
TO_CORE = [(seq_id(y, z, c), seq_id(y, z, c + 1)) for y in range(Y) for z in range(Z) for c in range(CORES)]


def to_x(steps):
    return [(y * X + x, y * X + (x + steps) % X) for y in range(YH) for x in range(X)]


def dot(a, b):
    return lax.dot_general(a, b, (((1,), (0,)), ((), ())), preferred_element_type=F32)


def causal():
    keys = lax.broadcasted_iota(jnp.int32, (ROWS, ROWS), 0)
    queries = lax.broadcasted_iota(jnp.int32, (ROWS, ROWS), 1)
    return keys <= queries


def weights_of(values):
    return jnp.concatenate([values.T, jnp.ones((ONES, values.shape[0]), BF16)], axis=0)


def add_keys(qt, acc, keys, values, masked=False, depth=2):
    weights = weights_of(values)
    scores = [dot(keys, qt[h]) for h in range(depth)]
    for h in range(H):
        p = jnp.exp2(scores.pop(0) * FACTOR2)
        if masked:
            p = jnp.where(causal(), p, 0.0)
        p = p.astype(BF16)
        if h + depth < H:
            scores.append(dot(keys, qt[h + depth]))
        acc[h] += dot(weights, p)


def safe_attention(qt, acc, top, read, parts, own):
    acc[...] = jnp.zeros_like(acc)
    top[...] = jnp.full_like(top, -1e30)

    def scores_of(keys, h, masked):
        s = dot(keys, qt[h]) * FACTOR
        return jnp.where(causal(), s, -1e30) if masked else s

    def find(keys, values, masked):
        def head(h, _):
            s = scores_of(keys, h, masked)
            top[h] = jnp.maximum(top[h], jnp.max(s, axis=0, keepdims=True))
            return 0

        lax.fori_loop(0, H, head, 0)

    def add(keys, values, masked):
        weights = weights_of(values)

        def head(h, _):
            p = jnp.exp(scores_of(keys, h, masked) - top[h])
            acc[h] += dot(weights, p.astype(BF16))
            return 0

        lax.fori_loop(0, H, head, 0)

    for visit in (find, add):
        def one(j, _, visit=visit):
            visit(*read(j, 1), False)
            return 0

        lax.fori_loop(0, parts, one, 0)
        if own is not None:
            visit(own[0][...], own[1][...], True)


def attend(q_ref, acc, qt, top, parts, read, own):
    for h in range(H):
        qt[h] = q_ref[:, h * DH : (h + 1) * DH].T
    acc[...] = jnp.zeros_like(acc)
    top[...] = jnp.zeros_like(top)
    if own is not None:
        add_keys(qt, acc, own[0][...], own[1][...], masked=True, depth=4)

    def whole(i, _):
        add_keys(qt, acc, *read(i * GROUP, GROUP))
        return 0

    lax.fori_loop(0, parts // GROUP, whole, 0)
    size = GROUP // 2
    while size:
        @pl.when(parts // size % 2 == 1)
        def _(size=size):
            add_keys(qt, acc, *read(parts // (2 * size) * (2 * size), size), depth=4)

        size //= 2

    if own is None:
        @pl.when(parts == 0)
        def _():
            top[...] = jnp.full_like(top, -1e30)

    sums = acc[:, DH : DH + 1, :]
    good = jnp.logical_and(sums > LOW, sums < HIGH)
    worst = jnp.min(jnp.where(good, 1.0, 0.0))
    some = parts >= (1 if own is None else 0)

    @pl.when(jnp.logical_and(worst < 0.5, some))
    def _():
        safe_attention(qt, acc, top, read, parts, own)

    for h in range(H):
        acc[h, DH + ONES // 2 :] = jnp.broadcast_to(top[h], (ONES // 2, ROWS))


def list_blocks(place, block_pos, chosen, rows_of):
    me = place[0]
    my_y, my_core = me // (Z * CORES), me % CORES

    def listed(i, count):
        source = (my_y + i % Y) % Y * (Z * CORES) + i // Y * CORES + my_core
        keep = block_pos[source] < block_pos[rows_of]

        @pl.when(keep)
        def _():
            chosen[count] = i

        return count + keep.astype(jnp.int32)

    return lax.fori_loop(0, Y * Z, listed, 0)


def self_kernel(place, block_pos, q_ref, partner_ref, kv, mine, theirs, qt, top, chosen):
    def read(first, number):
        blocks = [chosen[first + i] for i in range(number)]
        return tuple(jnp.concatenate([kv[b // Y, b % Y, which] for b in blocks], axis=0) for which in (0, 1))

    me = place[0]
    partner = me + 1 - 2 * (me % CORES)
    attend(partner_ref, theirs, qt, top, list_blocks(place, block_pos, chosen, partner), read, None)
    my_z = me // CORES % Z
    own = (kv.at[my_z, 0, 0], kv.at[my_z, 0, 1])
    attend(q_ref, mine, qt, top, list_blocks(place, block_pos, chosen, me), read, own)


def cross_kernel(partner, place, block_pos, mask, q_ref, *refs):
    columns, (out, qt, top, keys, values) = refs[:X], refs[X:]
    me = place[0]
    row = block_pos[me + 1 - 2 * (me % CORES) if partner else me]
    my_x = place[1] % X
    parts = jnp.int32(0)
    for column, shift in zip(columns, COLUMN_SHIFTS):
        for y in range(YH):
            keep = mask[row, y * X + (my_x + shift) % X] > 0

            @pl.when(keep)
            def _(column=column, y=y, parts=parts):
                at = pl.ds(pl.multiple_of(parts * ROWS, ROWS), ROWS)
                keys[at] = column[y, :, 0].reshape(ROWS, DH)
                values[at] = column[y, :, 1].reshape(ROWS, DH)

            parts = parts + keep.astype(jnp.int32)

    def read(first, number):
        at = pl.ds(pl.multiple_of(first * ROWS, ROWS), number * ROWS)
        return keys[at], values[at]

    attend(q_ref, out, qt, top, parts, read, None)


def join_kernel(mine, theirs, o_ref):
    for h in range(H):
        shifts = [part[h, DH + ONES // 2 : DH + ONES // 2 + 1] for part in (mine, theirs)]
        common = jnp.maximum(*shifts)
        scales = [jnp.exp(shift - common) for shift in shifts]
        total = sum(part[h, DH : DH + 1] * scale for part, scale in zip((mine, theirs), scales))
        rows = sum(part[h, :DH] * (scale / total) for part, scale in zip((mine, theirs), scales))
        o_ref[:, h * DH : (h + 1) * DH] = rows.astype(BF16).T


SUMS = jax.ShapeDtypeStruct((H, DH + ONES, ROWS), F32)
WORK = [pltpu.VMEM((H, DH, ROWS), BF16), pltpu.VMEM((H, 1, ROWS), F32)]


def call(kernel, name, scalars, arrays, outs, scratch, units):
    return pl.pallas_call(
        kernel,
        out_shape=outs,
        in_specs=[pl.BlockSpec(memory_space=pltpu.SMEM)] * len(scalars)
        + [pl.BlockSpec(memory_space=pltpu.VMEM)] * len(arrays),
        out_specs=jax.tree.map(lambda _: pl.BlockSpec(memory_space=pltpu.VMEM), outs),
        scratch_shapes=scratch,
        compiler_params=pltpu.CompilerParams(vmem_limit_bytes=32 * 2**20),
        cost_estimate=pl.CostEstimate(
            flops=units * 8 * H * ROWS * ROWS * DH, bytes_accessed=4 * 2**20, transcendentals=units * H * ROWS * ROWS
        ),
        name=name,
    )(*scalars, *arrays)


def spread(x, axis, groups):
    return lax.all_to_all(jnp.broadcast_to(x, (len(groups[0]), *x.shape)), axis, 0, 0, axis_index_groups=groups)


def per_device(text_q, cross_q, text_k, text_v, frame_k, frame_v, block_pos, frame_mask):
    place = jnp.stack([lax.axis_index("seq"), lax.axis_index("grp")]).astype(jnp.int32)

    own = jnp.stack([text_k[0], text_v[0]])
    across = lax.ppermute(own, "seq", TO_Y)
    partner_q = lax.ppermute(text_q[0], "seq", TO_CORE)
    partner_cross_q = lax.ppermute(cross_q[0], "seq", TO_CORE)
    text = lax.all_gather(jnp.stack([own, across]), "seq", axis_index_groups=Z_GROUPS)

    piece = jnp.stack([frame_k[0], frame_v[0]])
    line = spread(piece, "seq", Z_GROUPS)
    column = spread(line, ("grp", "seq"), Y_GROUPS).reshape(YH, Y * Z, *piece.shape)
    columns = [column] + [lax.ppermute(column, "grp", to_x(-shift)) for shift in COLUMN_SHIFTS[1:]]

    mine, theirs = call(
        self_kernel, "own", [place, block_pos], [text_q[0], partner_q, text], (SUMS, SUMS),
        [*WORK, pltpu.SMEM((Y * Z,), jnp.int32)], 16,
    )
    self_theirs = lax.ppermute(theirs, "seq", TO_CORE)

    def cross(queries, partner):
        return call(
            functools.partial(cross_kernel, partner), "cross", [place, block_pos, frame_mask], [queries, *columns],
            SUMS, [*WORK, *[pltpu.VMEM((X * YH * ROWS, DH), BF16)] * 2], 5,
        )

    partner_cross_q, mine = lax.optimization_barrier((partner_cross_q, mine))
    cross_theirs = cross(partner_cross_q, True)
    own_cross_q, cross_theirs = lax.optimization_barrier((cross_q[0], cross_theirs))
    cross_theirs = lax.ppermute(cross_theirs, "seq", TO_CORE)
    cross_mine = cross(own_cross_q, False)

    def join(a, b):
        return call(join_kernel, "join", [], [a, b], jax.ShapeDtypeStruct((ROWS, H * DH), BF16), [], 1)

    self_out = join(mine, self_theirs)
    cross_out = join(cross_mine, cross_theirs)
    return self_out[None], cross_out[None]


def solution(mesh):
    rows = P("grp", "seq", None)
    return jax.shard_map(
        per_device,
        mesh=mesh,
        in_specs=(rows, rows, rows, rows, rows, rows, P(), P()),
        out_specs=(rows, rows),
        check_vma=False,
    )
```

```python
import functools

import jax
import jax.numpy as jnp
from jax import lax
from jax.experimental import pallas as pl
from jax.experimental.pallas import tpu as pltpu
from jax.sharding import PartitionSpec as P

H = 8
DH = 128
ROWS = 256
ONES = 16
FACTOR = DH**-0.5
FACTOR2 = FACTOR * 1.4426950408889634
LOW, HIGH = 1e-28, 1e28
F32, BF16 = jnp.float32, jnp.bfloat16

Y, Z, CORES = 2, 8, 2
YH, X = 4, 4
GROUP = 4
COLUMN_SHIFTS = (0, -1, 1, 2)


def seq_id(y, z, c):
    return (y % Y * Z + z % Z) * CORES + c % CORES


Z_GROUPS = [[seq_id(y, z, c) for z in range(Z)] for y in range(Y) for c in range(CORES)]
Y_GROUPS = [
    [(yh * X + x) * (Y * Z * CORES) + seq_id(y, z, c) for yh in range(YH) for y in range(Y)]
    for x in range(X)
    for z in range(Z)
    for c in range(CORES)
]
TO_Y = [(seq_id(y, z, c), seq_id(y + 1, z, c)) for y in range(Y) for z in range(Z) for c in range(CORES)]
TO_CORE = [(seq_id(y, z, c), seq_id(y, z, c + 1)) for y in range(Y) for z in range(Z) for c in range(CORES)]


def to_x(steps):
    return [(y * X + x, y * X + (x + steps) % X) for y in range(YH) for x in range(X)]


def dot(a, b):
    return lax.dot_general(a, b, (((1,), (0,)), ((), ())), preferred_element_type=F32)


def causal():
    keys = lax.broadcasted_iota(jnp.int32, (ROWS, ROWS), 0)
    queries = lax.broadcasted_iota(jnp.int32, (ROWS, ROWS), 1)
    return keys <= queries


def weights_of(values):
    return jnp.concatenate([values.T, jnp.ones((ONES, values.shape[0]), BF16)], axis=0)


def add_keys(qt, acc, keys, values, masked=False, depth=2):
    weights = weights_of(values)
    scores = [dot(keys, qt[h]) for h in range(depth)]
    for h in range(H):
        p = jnp.exp2(scores.pop(0) * FACTOR2)
        if masked:
            p = jnp.where(causal(), p, 0.0)
        p = p.astype(BF16)
        if h + depth < H:
            scores.append(dot(keys, qt[h + depth]))
        acc[h] += dot(weights, p)


def safe_attention(qt, acc, top, read, parts, own):
    acc[...] = jnp.zeros_like(acc)
    top[...] = jnp.full_like(top, -1e30)

    def scores_of(keys, h, masked):
        s = dot(keys, qt[h]) * FACTOR
        return jnp.where(causal(), s, -1e30) if masked else s

    def find(keys, values, masked):
        def head(h, _):
            s = scores_of(keys, h, masked)
            top[h] = jnp.maximum(top[h], jnp.max(s, axis=0, keepdims=True))
            return 0

        lax.fori_loop(0, H, head, 0)

    def add(keys, values, masked):
        weights = weights_of(values)

        def head(h, _):
            p = jnp.exp(scores_of(keys, h, masked) - top[h])
            acc[h] += dot(weights, p.astype(BF16))
            return 0

        lax.fori_loop(0, H, head, 0)

    for visit in (find, add):
        def one(j, _, visit=visit):
            visit(*read(j, 1), False)
            return 0

        lax.fori_loop(0, parts, one, 0)
        if own is not None:
            visit(own[0][...], own[1][...], True)


def attend(q_ref, acc, qt, top, parts, read, own):
    for h in range(H):
        qt[h] = q_ref[:, h * DH : (h + 1) * DH].T
    acc[...] = jnp.zeros_like(acc)
    top[...] = jnp.zeros_like(top)
    if own is not None:
        add_keys(qt, acc, own[0][...], own[1][...], masked=True, depth=4)

    def whole(i, _):
        add_keys(qt, acc, *read(i * GROUP, GROUP))
        return 0

    lax.fori_loop(0, parts // GROUP, whole, 0)
    size = GROUP // 2
    while size:
        @pl.when(parts // size % 2 == 1)
        def _(size=size):
            add_keys(qt, acc, *read(parts // (2 * size) * (2 * size), size), depth=4)

        size //= 2

    if own is None:
        @pl.when(parts == 0)
        def _():
            top[...] = jnp.full_like(top, -1e30)

    sums = acc[:, DH : DH + 1, :]
    good = jnp.logical_and(sums > LOW, sums < HIGH)
    worst = jnp.min(jnp.where(good, 1.0, 0.0))
    some = parts >= (1 if own is None else 0)

    @pl.when(jnp.logical_and(worst < 0.5, some))
    def _():
        safe_attention(qt, acc, top, read, parts, own)

    for h in range(H):
        acc[h, DH + ONES // 2 :] = jnp.broadcast_to(top[h], (ONES // 2, ROWS))


def list_blocks(place, block_pos, chosen, rows_of):
    me = place[0]
    my_y, my_core = me // (Z * CORES), me % CORES

    def listed(i, count):
        source = (my_y + i % Y) % Y * (Z * CORES) + i // Y * CORES + my_core
        keep = block_pos[source] < block_pos[rows_of]

        @pl.when(keep)
        def _():
            chosen[count] = i

        return count + keep.astype(jnp.int32)

    return lax.fori_loop(0, Y * Z, listed, 0)


def self_kernel(place, block_pos, q_ref, partner_ref, kv, mine, theirs, qt, top, chosen):
    def read(first, number):
        blocks = [chosen[first + i] for i in range(number)]
        return tuple(jnp.concatenate([kv[b // Y, b % Y, which] for b in blocks], axis=0) for which in (0, 1))

    me = place[0]
    partner = me + 1 - 2 * (me % CORES)
    attend(partner_ref, theirs, qt, top, list_blocks(place, block_pos, chosen, partner), read, None)
    my_z = me // CORES % Z
    own = (kv.at[my_z, 0, 0], kv.at[my_z, 0, 1])
    attend(q_ref, mine, qt, top, list_blocks(place, block_pos, chosen, me), read, own)


def cross_kernel(place, block_pos, mask, q_ref, partner_ref, *refs):
    columns, (mine, theirs, qt, top, keys, values) = refs[:X], refs[X:]
    me = place[0]
    my_x = place[1] % X

    def read(first, number):
        at = pl.ds(pl.multiple_of(first * ROWS, ROWS), number * ROWS)
        return keys[at], values[at]

    for queries, out, owner in ((partner_ref, theirs, me + 1 - 2 * (me % CORES)), (q_ref, mine, me)):
        row, parts = block_pos[owner], jnp.int32(0)
        for column, shift in zip(columns, COLUMN_SHIFTS):
            for y in range(YH):
                keep = mask[row, y * X + (my_x + shift + X) % X] > 0

                @pl.when(keep)
                def _(column=column, y=y, parts=parts):
                    at = pl.ds(pl.multiple_of(parts * ROWS, ROWS), ROWS)
                    keys[at] = column[y, :, 0].reshape(ROWS, DH)
                    values[at] = column[y, :, 1].reshape(ROWS, DH)

                parts = parts + keep.astype(jnp.int32)
        attend(queries, out, qt, top, parts, read, None)


def join_kernel(self_mine, self_theirs, cross_mine, cross_theirs, self_out, cross_out):
    join(self_mine, self_theirs, self_out)
    join(cross_mine, cross_theirs, cross_out)


def join(mine, theirs, o_ref):
    for h in range(H):
        shifts = [part[h, DH + ONES // 2 : DH + ONES // 2 + 1] for part in (mine, theirs)]
        common = jnp.maximum(*shifts)
        scales = [jnp.exp(shift - common) for shift in shifts]
        total = sum(part[h, DH : DH + 1] * scale for part, scale in zip((mine, theirs), scales))
        rows = sum(part[h, :DH] * (scale / total) for part, scale in zip((mine, theirs), scales))
        o_ref[:, h * DH : (h + 1) * DH] = rows.astype(BF16).T


SUMS = jax.ShapeDtypeStruct((H, DH + ONES, ROWS), F32)
WORK = [pltpu.VMEM((H, DH, ROWS), BF16), pltpu.VMEM((H, 1, ROWS), F32)]


def call(kernel, name, scalars, arrays, outs, scratch, units):
    return pl.pallas_call(
        kernel,
        out_shape=outs,
        in_specs=[pl.BlockSpec(memory_space=pltpu.SMEM)] * len(scalars)
        + [pl.BlockSpec(memory_space=pltpu.VMEM)] * len(arrays),
        out_specs=jax.tree.map(lambda _: pl.BlockSpec(memory_space=pltpu.VMEM), outs),
        scratch_shapes=scratch,
        compiler_params=pltpu.CompilerParams(vmem_limit_bytes=32 * 2**20),
        cost_estimate=pl.CostEstimate(
            flops=units * 8 * H * ROWS * ROWS * DH, bytes_accessed=4 * 2**20, transcendentals=units * H * ROWS * ROWS
        ),
        name=name,
    )(*scalars, *arrays)


def spread(x, axis, groups):
    return lax.all_to_all(jnp.broadcast_to(x, (len(groups[0]), *x.shape)), axis, 0, 0, axis_index_groups=groups)


def per_device(text_q, cross_q, text_k, text_v, frame_k, frame_v, block_pos, frame_mask):
    place = jnp.stack([lax.axis_index("seq"), lax.axis_index("grp")]).astype(jnp.int32)

    own = jnp.stack([text_k[0], text_v[0]])
    across = lax.ppermute(own, "seq", TO_Y)
    partner_q = lax.ppermute(text_q[0], "seq", TO_CORE)
    partner_cross_q = lax.ppermute(cross_q[0], "seq", TO_CORE)
    text = lax.all_gather(jnp.stack([own, across]), "seq", axis_index_groups=Z_GROUPS)

    piece = jnp.stack([frame_k[0], frame_v[0]])
    line = spread(piece, "seq", Z_GROUPS)
    column = spread(line, ("grp", "seq"), Y_GROUPS).reshape(YH, Y * Z, *piece.shape)
    columns = [column] + [lax.ppermute(column, "grp", to_x(-shift)) for shift in COLUMN_SHIFTS[1:]]

    mine, theirs = call(
        self_kernel, "own", [place, block_pos], [text_q[0], partner_q, text], (SUMS, SUMS),
        [*WORK, pltpu.SMEM((Y * Z,), jnp.int32)], 16,
    )
    self_theirs = lax.ppermute(theirs, "seq", TO_CORE)
    own_cross_q, mine = lax.optimization_barrier((cross_q[0], mine))
    cross_mine, cross_theirs = call(
        cross_kernel, "cross", [place, block_pos, frame_mask], [own_cross_q, partner_cross_q, *columns],
        (SUMS, SUMS), [*WORK, *[pltpu.VMEM((X * YH * ROWS, DH), BF16)] * 2], 10,
    )
    cross_theirs = lax.ppermute(cross_theirs, "seq", TO_CORE)
    result = jax.ShapeDtypeStruct((ROWS, H * DH), BF16)
    self_out, cross_out = call(
        join_kernel, "join", [], [mine, self_theirs, cross_mine, cross_theirs], (result, result), [], 1
    )
    return self_out[None], cross_out[None]


def solution(mesh):
    rows = P("grp", "seq", None)
    return jax.shard_map(
        per_device,
        mesh=mesh,
        in_specs=(rows, rows, rows, rows, rows, rows, P(), P()),
        out_specs=(rows, rows),
        check_vma=False,
    )
```
